32 devices in a mesh: dp: 2 (over x), ctx: 16 (over z, y, core).
Axes of the slice: x: 2, y: 2, z: 4, core: 2. Of those that a mesh axis runs over, the one named last changes fastest.
Arguments:
- queries: bfloat16 [4096, 1024], P(('dp', 'ctx')), parts along dimension 0, may hold values from -8 to 8
- keys: bfloat16 [4096, 1024], P(('dp', 'ctx')), parts along dimension 0, may hold values from -8 to 8
- values: bfloat16 [4096, 1024], P(('dp', 'ctx')), parts along dimension 0, may hold values from -6 to 6
- grad_out: bfloat16 [4096, 1024], P(('dp', 'ctx')), parts along dimension 0, may hold values from -6 to 6
- rand_blocks: int32 [64, 3], P(('dp', 'ctx')), parts along dimension 0, may hold values from 0 to 1
- global_ids: int32 [4], P('dp'), parts along dimension 0, may hold values from 0 to 31
Outputs:
- attended: bfloat16 [4096, 1024], P(('dp', 'ctx')), parts along dimension 0
- grad_queries: bfloat16 [4096, 1024], P(('dp', 'ctx')), parts along dimension 0
- grad_keys: bfloat16 [4096, 1024], P(('dp', 'ctx')), parts along dimension 0
- grad_values: bfloat16 [4096, 1024], P(('dp', 'ctx')), parts along dimension 0
The draws below stay inside these ranges and needn't reach their ends.
There are 2 independent parts, one for each index of `dp`. The reference program is written for one: setup_inputs(seed, part) draws one part's arguments, and reference() takes and returns one part's arrays. A program takes and returns all parts, laid end to end along the dimension named above; each array names one. Nothing has to cross between parts.
All inputs are finite; a program needn't handle non-finite values.
Results may differ from the reference program's by a relative error of at most 0.02.
Values may be sent and summed in bfloat16 or wider, within the bound.
A program may use at most 128 MiB of HBM per device.

```python
import jax
import jax.numpy as jnp
from jax import lax

HEADS = 16
HEAD_DIM = 64
BLOCK = 64
RAND = 3
GLOBALS = 2
TOK_DEV = 128
D = 1024
SEQ = 2048
BLOCKS_DEV = 2
SEQ_BLOCKS = 32
N_CTX = 16


def paired_draw(key):
    first = jax.random.fold_in(key, 101)
    second = jax.random.fold_in(key, 202)
    query_field = jnp.clip(jax.random.normal(first, (SEQ, D), jnp.float32), -4.0, 4.0)
    key_field = jnp.clip(jax.random.normal(second, (SEQ, D), jnp.float32), -4.0, 4.0)
    return (query_field, key_field)


def draw_queries(key, part):
    return paired_draw(key)[0].astype(jnp.bfloat16)


def draw_keys(key, part):
    return paired_draw(key)[1].astype(jnp.bfloat16)


def with_ends(result, stream_key, least, largest):
    longest = result.shape.index(max(result.shape))
    spots = []
    for shift in (0, 1):
        where = [jax.random.randint(jax.random.fold_in(stream_key, axis), (), 0, length) for axis, length in enumerate(result.shape)]
        where[longest] = (where[longest] + shift) % result.shape[longest]
        spots.append(tuple(where))
    return result.at[spots[0]].set(least).at[spots[1]].set(largest)


def levels(stream_key, shape, split, smallest, high):
    factor_of = 1.0
    for position, parts in split:
        draws = jax.random.uniform(jax.random.fold_in(jax.random.fold_in(stream_key, 6), position), (parts,), jnp.float32, smallest / len(split), high / len(split))
        factor_of = factor_of * jnp.repeat(jnp.exp(draws), shape[position] // parts).reshape((-1,) + (1,) * (len(shape) - 1 - position))
    return factor_of


def scatter_about(rng, shape, deviation, reach, cuts=(), kind=jnp.bfloat16):
    array = jax.random.normal(rng, shape, jnp.float32) * deviation
    if len(cuts) > 0:
        array = levels(rng, shape, cuts, -0.22, 0.18) * array
    return jnp.clip(array, min=-reach, max=reach).astype(kind)


def setup_inputs(seed: int = 0, part: int = 0) -> dict:
    streams_of = jax.random.split(jax.random.key(seed), 7)
    part_splits = jax.random.split(jax.random.fold_in(streams_of[6], part), 7)
    return {
        "queries": draw_queries(jax.random.fold_in(jax.random.fold_in(streams_of[6], part), 71), part),
        "keys": draw_keys(jax.random.fold_in(jax.random.fold_in(streams_of[6], part), 71), part),
        "values": scatter_about(part_splits[2], (SEQ, D), 1.0, 6.0, ((0, 16),)),
        "grad_out": scatter_about(part_splits[3], (SEQ, D), 1.0, 6.0, ((0, 16),)),
        "rand_blocks": with_ends(jax.random.randint(part_splits[4], (SEQ_BLOCKS, RAND), 0, BLOCKS_DEV), jax.random.fold_in(part_splits[4], 1), 0, BLOCKS_DEV - 1).astype(jnp.int32),
        "global_ids": jax.random.randint(part_splits[5], (GLOBALS,), 0, SEQ_BLOCKS).astype(jnp.int32),
    }


SCORE_FLOOR = -1.0e30


def attend_blocks(query_blocks, key_blocks, value_blocks, grad_blocks, key_valid):
    scale_factor = HEAD_DIM ** -0.5
    query_wide = query_blocks.astype(jnp.float32)
    key_wide = key_blocks.astype(jnp.float32)
    value_wide = value_blocks.astype(jnp.float32)
    grad_wide = grad_blocks.astype(jnp.float32)
    scores = jnp.einsum("jqhd,jkhd->jhqk", query_wide, key_wide) * scale_factor
    scores = jnp.where(key_valid[:, None, None, :], scores, SCORE_FLOOR)
    highest = jnp.max(scores, axis=-1, keepdims=True)
    raw_weights = jnp.exp(scores - highest)
    probs = raw_weights / jnp.sum(raw_weights, axis=-1, keepdims=True)
    probs_low = probs.astype(jnp.bfloat16).astype(jnp.float32)
    attended = jnp.einsum("jhqk,jkhd->jqhd", probs_low, value_wide)
    grad_probs = jnp.einsum("jqhd,jkhd->jhqk", grad_wide, value_wide)
    inner = jnp.sum(probs * grad_probs, axis=-1, keepdims=True)
    grad_scores = (scale_factor * probs * (grad_probs - inner)).astype(jnp.bfloat16).astype(jnp.float32)
    grad_query = jnp.einsum("jhqk,jkhd->jqhd", grad_scores, key_wide)
    grad_key = jnp.einsum("jhqk,jqhd->jkhd", grad_scores, query_wide)
    grad_value = jnp.einsum("jhqk,jqhd->jkhd", probs_low, grad_wide)
    return attended, grad_query, grad_key, grad_value


def reference(queries, keys, values, grad_out, rand_blocks, global_ids):
    seq_rows, width = queries.shape
    seq_blocks = seq_rows // BLOCK
    dev_blocks = TOK_DEV // BLOCK
    listed = 3 + GLOBALS + RAND
    block_iota = jnp.arange(seq_blocks, dtype=jnp.int32)
    device_of = block_iota // dev_blocks
    columns = [jnp.clip(block_iota - 1, 0, seq_blocks - 1), block_iota, jnp.clip(block_iota + 1, 0, seq_blocks - 1)]
    for global_slot in range(GLOBALS):
        columns.append(jnp.broadcast_to(global_ids[global_slot], (seq_blocks,)).astype(jnp.int32))
    for matching in range(RAND):
        partner = jnp.bitwise_xor(device_of, jnp.int32(N_CTX // 2 ** (matching + 1)))
        columns.append((partner * dev_blocks + rand_blocks[:, matching]).astype(jnp.int32))
    table = jnp.stack(columns, axis=1).astype(jnp.int32)
    left_ok = block_iota > 0
    right_ok = block_iota < seq_blocks - 1
    stacked = jnp.stack([keys, values]).reshape(2, seq_blocks, BLOCK, width)
    listing_keep = jnp.concatenate([jnp.ones((3,), jnp.float32), jnp.zeros((GLOBALS,), jnp.float32), jnp.ones((RAND,), jnp.float32)])

    def one_slab(carry, slab):
        first = (slab * dev_blocks).astype(jnp.int32)
        rows = lax.dynamic_slice_in_dim(table, first, dev_blocks, 0)
        left_here = lax.dynamic_slice_in_dim(left_ok, first, dev_blocks, 0)
        right_here = lax.dynamic_slice_in_dim(right_ok, first, dev_blocks, 0)
        fill_true = jnp.ones((dev_blocks, BLOCK), dtype=bool)
        key_valid = jnp.concatenate(
            [jnp.broadcast_to(left_here[:, None], (dev_blocks, BLOCK)), fill_true,
             jnp.broadcast_to(right_here[:, None], (dev_blocks, BLOCK)),
             jnp.ones((dev_blocks, (GLOBALS + RAND) * BLOCK), dtype=bool)], axis=1)
        gathered = stacked[:, rows].reshape(2, dev_blocks, listed * BLOCK, HEADS, HEAD_DIM)
        start_row = (slab * TOK_DEV).astype(jnp.int32)
        query_blocks = lax.dynamic_slice_in_dim(queries, start_row, TOK_DEV, 0).reshape(dev_blocks, BLOCK, HEADS, HEAD_DIM)
        grad_blocks = lax.dynamic_slice_in_dim(grad_out, start_row, TOK_DEV, 0).reshape(dev_blocks, BLOCK, HEADS, HEAD_DIM)
        attended, grad_query, grad_key, grad_value = attend_blocks(query_blocks, gathered[0], gathered[1], grad_blocks, key_valid)
        terms = jnp.stack([grad_key, grad_value]).reshape(2, dev_blocks, listed, BLOCK, width)
        terms = terms * listing_keep[None, None, :, None, None]
        carry = carry.at[:, rows].add(terms)
        return carry, (attended.reshape(TOK_DEV, width).astype(jnp.bfloat16), grad_query.reshape(TOK_DEV, width).astype(jnp.bfloat16))

    start = jnp.zeros((2, seq_blocks, BLOCK, width), jnp.float32)
    totals, (attended, grad_query) = lax.scan(one_slab, start, jnp.arange(N_CTX, dtype=jnp.int32))
    grad_keys = totals[0].reshape(seq_rows, width).astype(jnp.bfloat16)
    grad_values = totals[1].reshape(seq_rows, width).astype(jnp.bfloat16)
    return attended.reshape(seq_rows, width), grad_query.reshape(seq_rows, width), grad_keys, grad_values
```

```python
import functools

import jax
import jax.numpy as jnp
from jax import lax
from jax.experimental import pallas as pl
from jax.experimental.pallas import tpu as pltpu
from jax.sharding import PartitionSpec as P

HEADS = 16
HEAD_DIM = 64
BLOCK = 64
RAND = 3
GLOBALS = 2
SLAB = 2 * BLOCK
PACK = 2 * HEAD_DIM
EXTRA = 16
SCORE_FLOOR = -1e30


def kernel(
    n,
    q_ref,
    k_ref,
    v_ref,
    g_ref,
    rand_ref,
    gid_ref,
    att_ref,
    dq_ref,
    dk_ref,
    dv_ref,
    a_pack,
    b_pack,
    a_all,
    b_all,
    acc,
    o_send,
    o_all,
    d_send,
    d_all,
    sem_as,
    sem_ar,
    sem_bs,
    sem_br,
    sem_os,
    sem_or,
    sem_ds,
    sem_dr,
):
    share = n // HEADS
    me = lax.axis_index("ctx")
    my_head = me // share
    my_turn = me % share

    def send_a(dest, origin):
        return pltpu.make_async_remote_copy(
            src_ref=a_pack.at[dest // share],
            dst_ref=a_all.at[pl.ds(2 * origin, 2)],
            send_sem=sem_as.at[dest],
            recv_sem=sem_ar.at[origin],
            device_id={"ctx": dest},
            device_id_type=pl.DeviceIdType.MESH,
        )

    def send_b(dest, origin):
        return pltpu.make_async_remote_copy(
            src_ref=b_pack.at[dest // share],
            dst_ref=b_all.at[origin],
            send_sem=sem_bs.at[dest],
            recv_sem=sem_br.at[origin],
            device_id={"ctx": dest},
            device_id_type=pl.DeviceIdType.MESH,
        )

    def send_o(dest, head):
        return pltpu.make_async_remote_copy(
            src_ref=o_send.at[dest],
            dst_ref=o_all.at[head],
            send_sem=sem_os.at[dest],
            recv_sem=sem_or.at[head],
            device_id={"ctx": dest},
            device_id_type=pl.DeviceIdType.MESH,
        )

    def send_d(dest, head):
        return pltpu.make_async_remote_copy(
            src_ref=d_send.at[dest],
            dst_ref=d_all.at[head],
            send_sem=sem_ds.at[dest],
            recv_sem=sem_dr.at[head],
            device_id={"ctx": dest},
            device_id_type=pl.DeviceIdType.MESH,
        )

    barrier = pltpu.get_barrier_semaphore()

    def greet(i, carry):
        pl.semaphore_signal(
            barrier,
            inc=1,
            device_id={"ctx": (me + i) % n},
            device_id_type=pl.DeviceIdType.MESH,
        )
        return carry

    lax.fori_loop(1, n, greet, 0)

    for pair in range(HEADS // 2):
        cols = slice(PACK * pair, PACK * (pair + 1))
        kt, vt = k_ref[:, cols], v_ref[:, cols]
        for odd in range(2):
            half = slice(HEAD_DIM * odd, HEAD_DIM * (odd + 1))
            both = jnp.concatenate([kt[:, half], vt[:, half]], axis=1)
            a_pack[2 * pair + odd] = both.reshape(2, BLOCK, PACK)
    pl.semaphore_wait(barrier, n - 1)

    def start_a(i, carry):
        send_a((me + i) % n, me).start()
        return carry

    lax.fori_loop(1, n, start_a, 0)

    lane = lax.broadcasted_iota(jnp.int32, (1, SLAB), 1)
    low = lane < BLOCK
    rows = [
        jnp.where(low, rand_ref[0, r], rand_ref[1, r]).astype(jnp.float32)
        for r in range(RAND)
    ]
    rows.append(jnp.zeros((EXTRA - RAND, SLAB), jnp.float32))
    picks = jnp.concatenate(rows, axis=0).astype(jnp.bfloat16)
    for pair in range(HEADS // 2):
        cols = slice(PACK * pair, PACK * (pair + 1))
        qt, gt = q_ref[:, cols], g_ref[:, cols]
        for odd in range(2):
            half = slice(HEAD_DIM * odd, HEAD_DIM * (odd + 1))
            b_pack[2 * pair + odd, :SLAB] = jnp.concatenate(
                [qt[:, half], gt[:, half]], axis=1
            )
            b_pack[2 * pair + odd, SLAB:] = picks

    def start_b(i, carry):
        send_b((me + i) % n, me).start()
        return carry

    lax.fori_loop(1, n, start_b, 0)

    a_all[pl.ds(2 * me, 2)] = a_pack[my_head]
    b_all[me] = b_pack[my_head]
    acc[...] = jnp.zeros_like(acc)

    def arrive_a(i, carry):
        send_a(me, (me + n - i) % n).wait_recv()
        return carry

    lax.fori_loop(1, n, arrive_a, 0)

    lane_f = jnp.where(low, 0.125, 0.0)
    keep_q = lane_f.astype(jnp.bfloat16)
    keep_g = jnp.where(low, 0.0, 1.0).astype(jnp.bfloat16)
    fixed = [a_all[gid_ref[slot]] for slot in range(GLOBALS)]

    def partner(c, r):
        d = n // 2 ** (r + 1)
        return c + d - 2 * d * ((c // d) % 2)

    def slab(c):
        mixed = b_all[c]
        tokens = mixed[:SLAB]
        both = jnp.concatenate([tokens * keep_q, tokens * keep_g], axis=0)
        before = jnp.maximum(2 * c - 1, 0)
        after = jnp.minimum(2 * c + 2, 2 * n - 1)
        listed = [a_all[before], a_all[2 * c], a_all[2 * c + 1], a_all[after]]
        for r in range(RAND):
            other = partner(c, r)
            listed += [a_all[2 * other], a_all[2 * other + 1]]
        own_rows = len(listed) * BLOCK
        keys = jnp.concatenate(listed + fixed, axis=0)
        prod = lax.dot_general(
            keys, both, (((1,), (1,)), ((), ())), preferred_element_type=jnp.float32
        )
        scores = prod[:, :SLAB]
        grads = prod[:, SLAB:]
        chosen = mixed[SLAB:].astype(jnp.float32)
        segs = [scores[i * BLOCK : (i + 1) * BLOCK] for i in range(len(listed))]
        left_ok = lane + jnp.where(c > 0, 0, SLAB) < BLOCK
        right_ok = lane - jnp.where(c < n - 1, 0, SLAB) >= BLOCK
        segs[0] = jnp.where(left_ok, segs[0], SCORE_FLOOR)
        segs[3] = jnp.where(right_ok, segs[3], SCORE_FLOOR)
        for r in range(RAND):
            pick = chosen[r : r + 1]
            segs[4 + 2 * r] = jnp.where(pick < 0.5, segs[4 + 2 * r], SCORE_FLOOR)
            segs[5 + 2 * r] = jnp.where(pick > 0.5, segs[5 + 2 * r], SCORE_FLOOR)
        scores = jnp.concatenate(segs + [scores[own_rows:]], axis=0)
        highest = jnp.max(scores, axis=0, keepdims=True)
        raw = jnp.exp(scores - highest)
        inverse = 1.0 / jnp.sum(raw, axis=0, keepdims=True)
        inner = jnp.sum(raw * grads, axis=0, keepdims=True) * inverse
        probs = raw * inverse
        grad_scores = probs * (grads - inner)
        packed = jnp.concatenate(
            [grad_scores.astype(jnp.bfloat16), probs.astype(jnp.bfloat16)], axis=1
        )
        terms = jnp.dot(packed[:own_rows], both, preferred_element_type=jnp.float32)
        out = lax.dot_general(
            keys, packed, (((0,), (0,)), ((), ())), preferred_element_type=jnp.float32
        )
        out = jnp.concatenate(
            [out[:HEAD_DIM, :SLAB] * 0.125, out[HEAD_DIM:, SLAB:]], axis=0
        )
        o_send[c] = out.T.astype(jnp.bfloat16)
        places = [before, 2 * c, 2 * c + 1, after]
        for r in range(RAND):
            other = partner(c, r)
            places += [2 * other, 2 * other + 1]
        for i, place in enumerate(places):
            acc[place] += terms[i * BLOCK : (i + 1) * BLOCK]

    def return_o(c):
        if share == 1:
            send_o(c, my_head).start()
        else:

            @pl.when(c % share == my_turn)
            def _():
                send_o(c, my_head).start()

    slab(me)
    o_all[my_head] = o_send[me]

    def step(i, carry):
        c = (me + n - i) % n
        send_b(me, c).wait_recv()
        slab(c)
        return_o(c)
        return carry

    lax.fori_loop(1, n, step, 0)

    def return_d(i, carry):
        c = ((my_head + HEADS - i) % HEADS) * share + my_turn
        d_send[c] = acc[pl.ds(2 * c, 2)].reshape(SLAB, PACK).astype(jnp.bfloat16)
        send_d(c, my_head).start()
        return carry

    lax.fori_loop(1, HEADS, return_d, 0)
    d_all[my_head] = acc[pl.ds(2 * me, 2)].reshape(SLAB, PACK).astype(jnp.bfloat16)

    def arrive_o(i, carry):
        send_o(me, (my_head + i) % HEADS).wait_recv()
        return carry

    lax.fori_loop(1, HEADS, arrive_o, 0)

    def unpack(source, low_ref, high_ref):
        for pair in range(HEADS // 2):
            cols = slice(PACK * pair, PACK * (pair + 1))
            even, odd = source[2 * pair], source[2 * pair + 1]
            low_ref[:, cols] = jnp.concatenate(
                [even[:, :HEAD_DIM], odd[:, :HEAD_DIM]], axis=1
            )
            high_ref[:, cols] = jnp.concatenate(
                [even[:, HEAD_DIM:], odd[:, HEAD_DIM:]], axis=1
            )

    unpack(o_all, dq_ref, att_ref)

    def arrive_d(i, carry):
        send_d(me, (my_head + i) % HEADS).wait_recv()
        return carry

    lax.fori_loop(1, HEADS, arrive_d, 0)
    unpack(d_all, dk_ref, dv_ref)

    def sent_in(i, carry):
        send_a((me + i) % n, me).wait_send()
        send_b((me + i) % n, me).wait_send()
        return carry

    lax.fori_loop(1, n, sent_in, 0)

    def sent_back(i, carry):
        c = ((my_head + HEADS - i) % HEADS) * share + my_turn
        send_o(c, my_head).wait_send()
        send_d(c, my_head).wait_send()
        return carry

    lax.fori_loop(1, HEADS, sent_back, 0)


def local(n, queries, keys, values, grad_out, rand_blocks, global_ids):
    out = jax.ShapeDtypeStruct(queries.shape, jnp.bfloat16)
    vmem = pl.BlockSpec(memory_space=pltpu.VMEM)
    smem = pl.BlockSpec(memory_space=pltpu.SMEM)
    dma = pltpu.SemaphoreType.DMA
    return pl.pallas_call(
        functools.partial(kernel, n),
        out_shape=(out,) * 4,
        in_specs=[vmem] * 4 + [smem] * 2,
        out_specs=(vmem,) * 4,
        scratch_shapes=[
            pltpu.VMEM((HEADS, 2, BLOCK, PACK), jnp.bfloat16),
            pltpu.VMEM((HEADS, SLAB + EXTRA, PACK), jnp.bfloat16),
            pltpu.VMEM((2 * n, BLOCK, PACK), jnp.bfloat16),
            pltpu.VMEM((n, SLAB + EXTRA, PACK), jnp.bfloat16),
            pltpu.VMEM((2 * n, BLOCK, PACK), jnp.float32),
            pltpu.VMEM((n, SLAB, PACK), jnp.bfloat16),
            pltpu.VMEM((HEADS, SLAB, PACK), jnp.bfloat16),
            pltpu.VMEM((n, SLAB, PACK), jnp.bfloat16),
            pltpu.VMEM((HEADS, SLAB, PACK), jnp.bfloat16),
            dma((n,)),
            dma((n,)),
            dma((n,)),
            dma((n,)),
            dma((n,)),
            dma((HEADS,)),
            dma((n,)),
            dma((HEADS,)),
        ],
        compiler_params=pltpu.CompilerParams(
            collective_id=0, has_side_effects=True, vmem_limit_bytes=48 * 1024 * 1024
        ),
    )(queries, keys, values, grad_out, rand_blocks, global_ids)


def solution(mesh):
    rows = P(("dp", "ctx"), None)
    return jax.shard_map(
        functools.partial(local, mesh.shape["ctx"]),
        mesh=mesh,
        in_specs=(rows,) * 5 + (P("dp"),),
        out_specs=(rows,) * 4,
        check_vma=False,
    )
```

```python
import functools

import jax
import jax.numpy as jnp
from jax import lax
from jax.experimental import pallas as pl
from jax.experimental.pallas import tpu as pltpu
from jax.sharding import PartitionSpec as P

HEADS = 16
HEAD_DIM = 64
BLOCK = 64
RAND = 3
GLOBALS = 2
SLAB = 2 * BLOCK
PACK = 2 * HEAD_DIM
EXTRA = 16
SCORE_FLOOR = -1e30


def kernel(
    n,
    q_hbm,
    k_hbm,
    v_hbm,
    g_hbm,
    rand_hbm,
    gid_hbm,
    att_ref,
    dq_ref,
    dk_ref,
    dv_ref,
    q_ref,
    k_ref,
    v_ref,
    g_ref,
    rand_ref,
    gid_ref,
    sem_in,
    a_pack,
    b_pack,
    a_all,
    b_all,
    acc,
    o_send,
    o_all,
    d_send,
    d_all,
    sem_as,
    sem_ar,
    sem_bs,
    sem_br,
    sem_os,
    sem_or,
    sem_ds,
    sem_dr,
):
    share = n // HEADS
    me = lax.axis_index("ctx")
    my_head = me // share
    my_turn = me % share

    def send_a(dest, origin):
        return pltpu.make_async_remote_copy(
            src_ref=a_pack.at[dest // share],
            dst_ref=a_all.at[pl.ds(2 * origin, 2)],
            send_sem=sem_as.at[dest],
            recv_sem=sem_ar.at[origin],
            device_id={"ctx": dest},
            device_id_type=pl.DeviceIdType.MESH,
        )

    def send_b(dest, origin):
        return pltpu.make_async_remote_copy(
            src_ref=b_pack.at[dest // share],
            dst_ref=b_all.at[origin],
            send_sem=sem_bs.at[dest],
            recv_sem=sem_br.at[origin],
            device_id={"ctx": dest},
            device_id_type=pl.DeviceIdType.MESH,
        )

    def send_o(dest, head):
        return pltpu.make_async_remote_copy(
            src_ref=o_send.at[dest],
            dst_ref=o_all.at[head],
            send_sem=sem_os.at[dest],
            recv_sem=sem_or.at[head],
            device_id={"ctx": dest},
            device_id_type=pl.DeviceIdType.MESH,
        )

    def send_d(dest, head):
        return pltpu.make_async_remote_copy(
            src_ref=d_send.at[dest],
            dst_ref=d_all.at[head],
            send_sem=sem_ds.at[dest],
            recv_sem=sem_dr.at[head],
            device_id={"ctx": dest},
            device_id_type=pl.DeviceIdType.MESH,
        )

    pairs_in = (
        (k_hbm, k_ref),
        (v_hbm, v_ref),
        (q_hbm, q_ref),
        (g_hbm, g_ref),
        (rand_hbm, rand_ref),
        (gid_hbm, gid_ref),
    )
    fetches = [
        pltpu.make_async_copy(src, dst, sem_in.at[i])
        for i, (src, dst) in enumerate(pairs_in)
    ]
    for fetch in fetches:
        fetch.start()
    barrier = pltpu.get_barrier_semaphore()

    def greet(i, carry):
        pl.semaphore_signal(
            barrier,
            inc=1,
            device_id={"ctx": (me + i) % n},
            device_id_type=pl.DeviceIdType.MESH,
        )
        return carry

    lax.fori_loop(1, n, greet, 0)

    fetches[0].wait()
    fetches[1].wait()
    for pair in range(HEADS // 2):
        cols = slice(PACK * pair, PACK * (pair + 1))
        kt, vt = k_ref[:, cols], v_ref[:, cols]
        for odd in range(2):
            half = slice(HEAD_DIM * odd, HEAD_DIM * (odd + 1))
            both = jnp.concatenate([kt[:, half], vt[:, half]], axis=1)
            a_pack[2 * pair + odd] = both.reshape(2, BLOCK, PACK)
    pl.semaphore_wait(barrier, n - 1)

    def start_a(i, carry):
        send_a((me + i) % n, me).start()
        return carry

    lax.fori_loop(1, n, start_a, 0)

    for fetch in fetches[2:]:
        fetch.wait()
    lane = lax.broadcasted_iota(jnp.int32, (1, SLAB), 1)
    low = lane < BLOCK
    rows = [
        jnp.where(low, rand_ref[0, r], rand_ref[1, r]).astype(jnp.float32)
        for r in range(RAND)
    ]
    rows.append(jnp.zeros((EXTRA - RAND, SLAB), jnp.float32))
    picks = jnp.concatenate(rows, axis=0).astype(jnp.bfloat16)
    for pair in range(HEADS // 2):
        cols = slice(PACK * pair, PACK * (pair + 1))
        qt, gt = q_ref[:, cols], g_ref[:, cols]
        for odd in range(2):
            half = slice(HEAD_DIM * odd, HEAD_DIM * (odd + 1))
            b_pack[2 * pair + odd, :SLAB] = jnp.concatenate(
                [qt[:, half], gt[:, half]], axis=1
            )
            b_pack[2 * pair + odd, SLAB:] = picks

    def start_b(i, carry):
        send_b((me + i) % n, me).start()
        return carry

    lax.fori_loop(1, n, start_b, 0)

    a_all[pl.ds(2 * me, 2)] = a_pack[my_head]
    b_all[me] = b_pack[my_head]
    acc[...] = jnp.zeros_like(acc)

    def arrive_a(i, carry):
        send_a(me, (me + n - i) % n).wait_recv()
        return carry

    lax.fori_loop(1, n, arrive_a, 0)

    lane_f = jnp.where(low, 0.125, 0.0)
    keep_q = lane_f.astype(jnp.bfloat16)
    keep_g = jnp.where(low, 0.0, 1.0).astype(jnp.bfloat16)
    fixed = [a_all[gid_ref[slot]] for slot in range(GLOBALS)]

    def partner(c, r):
        d = n // 2 ** (r + 1)
        return c + d - 2 * d * ((c // d) % 2)

    def slab(c):
        mixed = b_all[c]
        tokens = mixed[:SLAB]
        both = jnp.concatenate([tokens * keep_q, tokens * keep_g], axis=0)
        before = jnp.maximum(2 * c - 1, 0)
        after = jnp.minimum(2 * c + 2, 2 * n - 1)
        listed = [a_all[before], a_all[2 * c], a_all[2 * c + 1], a_all[after]]
        for r in range(RAND):
            other = partner(c, r)
            listed += [a_all[2 * other], a_all[2 * other + 1]]
        own_rows = len(listed) * BLOCK
        keys = jnp.concatenate(listed + fixed, axis=0)
        prod = lax.dot_general(
            keys, both, (((1,), (1,)), ((), ())), preferred_element_type=jnp.float32
        )
        scores = prod[:, :SLAB]
        grads = prod[:, SLAB:]
        chosen = mixed[SLAB:].astype(jnp.float32)
        segs = [scores[i * BLOCK : (i + 1) * BLOCK] for i in range(len(listed))]
        left_ok = lane + jnp.where(c > 0, 0, SLAB) < BLOCK
        right_ok = lane - jnp.where(c < n - 1, 0, SLAB) >= BLOCK
        segs[0] = jnp.where(left_ok, segs[0], SCORE_FLOOR)
        segs[3] = jnp.where(right_ok, segs[3], SCORE_FLOOR)
        for r in range(RAND):
            pick = chosen[r : r + 1]
            segs[4 + 2 * r] = jnp.where(pick < 0.5, segs[4 + 2 * r], SCORE_FLOOR)
            segs[5 + 2 * r] = jnp.where(pick > 0.5, segs[5 + 2 * r], SCORE_FLOOR)
        scores = jnp.concatenate(segs + [scores[own_rows:]], axis=0)
        highest = jnp.max(scores, axis=0, keepdims=True)
        raw = jnp.exp(scores - highest)
        inverse = 1.0 / jnp.sum(raw, axis=0, keepdims=True)
        inner = jnp.sum(raw * grads, axis=0, keepdims=True) * inverse
        probs = raw * inverse
        grad_scores = probs * (grads - inner)
        packed = jnp.concatenate(
            [grad_scores.astype(jnp.bfloat16), probs.astype(jnp.bfloat16)], axis=1
        )
        terms = jnp.dot(packed[:own_rows], both, preferred_element_type=jnp.float32)
        out = lax.dot_general(
            keys, packed, (((0,), (0,)), ((), ())), preferred_element_type=jnp.float32
        )
        out = jnp.concatenate(
            [out[:HEAD_DIM, :SLAB] * 0.125, out[HEAD_DIM:, SLAB:]], axis=0
        )
        o_send[c] = out.T.astype(jnp.bfloat16)
        places = [before, 2 * c, 2 * c + 1, after]
        for r in range(RAND):
            other = partner(c, r)
            places += [2 * other, 2 * other + 1]
        return places, terms

    def add_terms(places, terms):
        for i, place in enumerate(places):
            acc[place] += terms[i * BLOCK : (i + 1) * BLOCK]

    half_n = n // 2
    my_pair = me // 2

    def arrive_b(c):
        @pl.when(c != me)
        def _():
            send_b(me, c).wait_recv()

    def return_o(c):
        @pl.when((c != me) & (c % share == my_turn))
        def _():
            send_o(c, my_head).start()

        @pl.when(c == me)
        def _():
            o_all[my_head] = o_send[me]

    def return_d(c):
        @pl.when((c != me) & (c % share == my_turn))
        def _():
            total = acc[pl.ds(2 * c, 2)].reshape(SLAB, PACK)
            d_send[c] = total.astype(jnp.bfloat16)
            send_d(c, my_head).start()

        @pl.when(c == me)
        def _():
            total = acc[pl.ds(2 * me, 2)].reshape(SLAB, PACK)
            d_all[my_head] = total.astype(jnp.bfloat16)

    def place_of(j, odd):
        return 2 * ((my_pair + half_n - j) % half_n) + odd

    def two_slabs(first, second):
        arrive_b(first)
        arrive_b(second)
        done = [slab(first), slab(second)]
        for places, terms in done:
            add_terms(places, terms)
        return_o(first)
        return_o(second)

    def even_step(t, carry):
        two_slabs(place_of(2 * t, 0), place_of(2 * t + 1, 0))
        return carry

    lax.fori_loop(0, half_n // 2, even_step, 0)

    def odd_step(t, carry):
        first, second = place_of(2 * t, 1), place_of(2 * t + 1, 1)
        two_slabs(first, second)

        @pl.when(t > 0)
        def _():
            return_d((first + 1) % n)

        return_d((second + 1) % n)
        return carry

    lax.fori_loop(0, half_n // 2, odd_step, 0)
    return_d((place_of(0, 1) + 1) % n)

    def return_odd(i, carry):
        return_d(place_of(i, 1))
        return carry

    lax.fori_loop(0, half_n, return_odd, 0)

    def arrive_o(i, carry):
        send_o(me, (my_head + i) % HEADS).wait_recv()
        return carry

    lax.fori_loop(1, HEADS, arrive_o, 0)

    def unpack(source, low_ref, high_ref):
        for pair in range(HEADS // 2):
            cols = slice(PACK * pair, PACK * (pair + 1))
            even, odd = source[2 * pair], source[2 * pair + 1]
            low_ref[:, cols] = jnp.concatenate(
                [even[:, :HEAD_DIM], odd[:, :HEAD_DIM]], axis=1
            )
            high_ref[:, cols] = jnp.concatenate(
                [even[:, HEAD_DIM:], odd[:, HEAD_DIM:]], axis=1
            )

    unpack(o_all, dq_ref, att_ref)

    def arrive_d(i, carry):
        send_d(me, (my_head + i) % HEADS).wait_recv()
        return carry

    lax.fori_loop(1, HEADS, arrive_d, 0)
    unpack(d_all, dk_ref, dv_ref)

    def sent_in(i, carry):
        send_a((me + i) % n, me).wait_send()
        send_b((me + i) % n, me).wait_send()
        return carry

    lax.fori_loop(1, n, sent_in, 0)

    def sent_back(i, carry):
        c = ((my_head + HEADS - i) % HEADS) * share + my_turn
        send_o(c, my_head).wait_send()
        send_d(c, my_head).wait_send()
        return carry

    lax.fori_loop(1, HEADS, sent_back, 0)


def local(n, queries, keys, values, grad_out, rand_blocks, global_ids):
    out = jax.ShapeDtypeStruct(queries.shape, jnp.bfloat16)
    vmem = pl.BlockSpec(memory_space=pltpu.VMEM)
    dma = pltpu.SemaphoreType.DMA
    return pl.pallas_call(
        functools.partial(kernel, n),
        out_shape=(out,) * 4,
        in_specs=[pl.BlockSpec(memory_space=pltpu.HBM)] * 6,
        out_specs=(vmem,) * 4,
        scratch_shapes=[
            pltpu.VMEM(queries.shape, jnp.bfloat16),
            pltpu.VMEM(queries.shape, jnp.bfloat16),
            pltpu.VMEM(queries.shape, jnp.bfloat16),
            pltpu.VMEM(queries.shape, jnp.bfloat16),
            pltpu.SMEM(rand_blocks.shape, jnp.int32),
            pltpu.SMEM(global_ids.shape, jnp.int32),
            dma((6,)),
            pltpu.VMEM((HEADS, 2, BLOCK, PACK), jnp.bfloat16),
            pltpu.VMEM((HEADS, SLAB + EXTRA, PACK), jnp.bfloat16),
            pltpu.VMEM((2 * n, BLOCK, PACK), jnp.bfloat16),
            pltpu.VMEM((n, SLAB + EXTRA, PACK), jnp.bfloat16),
            pltpu.VMEM((2 * n, BLOCK, PACK), jnp.float32),
            pltpu.VMEM((n, SLAB, PACK), jnp.bfloat16),
            pltpu.VMEM((HEADS, SLAB, PACK), jnp.bfloat16),
            pltpu.VMEM((n, SLAB, PACK), jnp.bfloat16),
            pltpu.VMEM((HEADS, SLAB, PACK), jnp.bfloat16),
            dma((n,)),
            dma((n,)),
            dma((n,)),
            dma((n,)),
            dma((n,)),
            dma((HEADS,)),
            dma((n,)),
            dma((HEADS,)),
        ],
        compiler_params=pltpu.CompilerParams(
            collective_id=0, has_side_effects=True, vmem_limit_bytes=48 * 1024 * 1024
        ),
    )(queries, keys, values, grad_out, rand_blocks, global_ids)


def solution(mesh):
    rows = P(("dp", "ctx"), None)
    return jax.shard_map(
        functools.partial(local, mesh.shape["ctx"]),
        mesh=mesh,
        in_specs=(rows,) * 5 + (P("dp"),),
        out_specs=(rows,) * 4,
        check_vma=False,
    )
```

```python
import functools

import jax
import jax.numpy as jnp
from jax import lax
from jax.experimental import pallas as pl
from jax.experimental.pallas import tpu as pltpu
from jax.sharding import PartitionSpec as P

HEADS = 16
HEAD_DIM = 64
BLOCK = 64
RAND = 3
GLOBALS = 2
SLAB = 2 * BLOCK
PACK = 2 * HEAD_DIM
SCORE_FLOOR = -1e30


def kernel(
    n,
    q_hbm,
    k_hbm,
    v_hbm,
    g_hbm,
    rand_hbm,
    gid_hbm,
    att_ref,
    dq_ref,
    dk_ref,
    dv_ref,
    q_ref,
    k_ref,
    v_ref,
    g_ref,
    rand_ref,
    gid_ref,
    sem_in,
    a_pack,
    b_pack,
    a_all,
    b_all,
    acc,
    o_send,
    o_all,
    d_send,
    d_all,
    c_pack,
    c_all,
    sem_cs,
    sem_cr,
    sem_as,
    sem_ar,
    sem_bs,
    sem_br,
    sem_os,
    sem_or,
    sem_ds,
    sem_dr,
):
    share = n // HEADS
    me = lax.axis_index("ctx")
    my_head = me // share
    my_turn = me % share

    def send_a(dest, origin):
        return pltpu.make_async_remote_copy(
            src_ref=a_pack.at[dest // share],
            dst_ref=a_all.at[pl.ds(2 * origin, 2)],
            send_sem=sem_as.at[dest],
            recv_sem=sem_ar.at[origin],
            device_id={"ctx": dest},
            device_id_type=pl.DeviceIdType.MESH,
        )

    def send_b(dest, origin):
        return pltpu.make_async_remote_copy(
            src_ref=b_pack.at[dest // share],
            dst_ref=b_all.at[origin],
            send_sem=sem_bs.at[dest],
            recv_sem=sem_br.at[origin],
            device_id={"ctx": dest},
            device_id_type=pl.DeviceIdType.MESH,
        )

    def send_c(dest, origin):
        return pltpu.make_async_remote_copy(
            src_ref=c_pack,
            dst_ref=c_all.at[origin],
            send_sem=sem_cs.at[dest],
            recv_sem=sem_cr.at[origin],
            device_id={"ctx": dest},
            device_id_type=pl.DeviceIdType.MESH,
        )

    half_n = n // 2
    side = me // half_n
    spot = me % half_n

    def far(t):
        return (1 - side) * half_n + (spot + t) % half_n

    def near(t):
        return side * half_n + (spot + t) % half_n

    def to_all(send):
        send(far(0), me).start()

        def body(t, carry):
            send(far(t), me).start()
            send(near(t), me).start()
            return carry

        lax.fori_loop(1, half_n, body, 0)

    def send_o(dest, head):
        return pltpu.make_async_remote_copy(
            src_ref=o_send.at[dest],
            dst_ref=o_all.at[head],
            send_sem=sem_os.at[dest],
            recv_sem=sem_or.at[head],
            device_id={"ctx": dest},
            device_id_type=pl.DeviceIdType.MESH,
        )

    def send_d(dest, head):
        return pltpu.make_async_remote_copy(
            src_ref=d_send.at[dest],
            dst_ref=d_all.at[head],
            send_sem=sem_ds.at[dest],
            recv_sem=sem_dr.at[head],
            device_id={"ctx": dest},
            device_id_type=pl.DeviceIdType.MESH,
        )

    pairs_in = (
        (k_hbm, k_ref),
        (v_hbm, v_ref),
        (q_hbm, q_ref),
        (g_hbm, g_ref),
        (rand_hbm, rand_ref),
        (gid_hbm, gid_ref),
    )
    fetches = [
        pltpu.make_async_copy(src, dst, sem_in.at[i])
        for i, (src, dst) in enumerate(pairs_in)
    ]
    for fetch in fetches:
        fetch.start()
    barrier = pltpu.get_barrier_semaphore()

    def greet(i, carry):
        pl.semaphore_signal(
            barrier,
            inc=1,
            device_id={"ctx": (me + i) % n},
            device_id_type=pl.DeviceIdType.MESH,
        )
        return carry

    lax.fori_loop(1, n, greet, 0)

    fetches[0].wait()
    fetches[1].wait()
    for pair in range(HEADS // 2):
        cols = slice(PACK * pair, PACK * (pair + 1))
        kt, vt = k_ref[:, cols], v_ref[:, cols]
        for odd in range(2):
            half = slice(HEAD_DIM * odd, HEAD_DIM * (odd + 1))
            both = jnp.concatenate([kt[:, half], vt[:, half]], axis=1)
            a_pack[2 * pair + odd] = both.reshape(2, BLOCK, PACK)
    pl.semaphore_wait(barrier, n - 1)

    to_all(send_a)

    for fetch in fetches[2:]:
        fetch.wait()
    lane = lax.broadcasted_iota(jnp.int32, (1, SLAB), 1)
    low = lane < BLOCK
    code = jnp.where(low, rand_ref[0, 0], rand_ref[1, 0])
    for r in range(1, RAND):
        code += jnp.where(low, rand_ref[0, r], rand_ref[1, r]) * 2**r
    c_pack[...] = code.astype(jnp.float32)
    for pair in range(HEADS // 2):
        cols = slice(PACK * pair, PACK * (pair + 1))
        qt, gt = q_ref[:, cols], g_ref[:, cols]
        for odd in range(2):
            half = slice(HEAD_DIM * odd, HEAD_DIM * (odd + 1))
            b_pack[2 * pair + odd] = jnp.concatenate(
                [qt[:, half], gt[:, half]], axis=1
            )

    to_all(send_c)
    to_all(send_b)

    a_all[pl.ds(2 * me, 2)] = a_pack[my_head]
    b_all[me] = b_pack[my_head]
    c_all[me] = c_pack[...]
    acc[...] = jnp.zeros_like(acc)

    def arrive_a(i, carry):
        send_a(me, (me + n - i) % n).wait_recv()
        send_c(me, (me + n - i) % n).wait_recv()
        return carry

    lax.fori_loop(1, n, arrive_a, 0)

    lane_f = jnp.where(low, 0.125, 0.0)
    keep_q = lane_f.astype(jnp.bfloat16)
    keep_g = jnp.where(low, 0.0, 1.0).astype(jnp.bfloat16)
    fixed = [a_all[gid_ref[slot]] for slot in range(GLOBALS)]

    def partner(c, r):
        d = n // 2 ** (r + 1)
        return c + d - 2 * d * ((c // d) % 2)

    def slab(c):
        tokens = b_all[c]
        both = jnp.concatenate([tokens * keep_q, tokens * keep_g], axis=0)
        before = jnp.maximum(2 * c - 1, 0)
        after = jnp.minimum(2 * c + 2, 2 * n - 1)
        listed = [a_all[before], a_all[2 * c], a_all[2 * c + 1], a_all[after]]
        for r in range(RAND):
            other = partner(c, r)
            listed += [a_all[2 * other], a_all[2 * other + 1]]
        own_rows = len(listed) * BLOCK
        keys = jnp.concatenate(listed + fixed, axis=0)
        prod = lax.dot_general(
            keys, both, (((1,), (1,)), ((), ())), preferred_element_type=jnp.float32
        )
        scores = prod[:, :SLAB]
        grads = prod[:, SLAB:]
        code = c_all[c].astype(jnp.int32)
        segs = [scores[i * BLOCK : (i + 1) * BLOCK] for i in range(len(listed))]
        left_ok = lane + jnp.where(c > 0, 0, SLAB) < BLOCK
        right_ok = lane - jnp.where(c < n - 1, 0, SLAB) >= BLOCK
        segs[0] = jnp.where(left_ok, segs[0], SCORE_FLOOR)
        segs[3] = jnp.where(right_ok, segs[3], SCORE_FLOOR)
        for r in range(RAND):
            pick = (code >> r) & 1
            segs[4 + 2 * r] = jnp.where(pick == 0, segs[4 + 2 * r], SCORE_FLOOR)
            segs[5 + 2 * r] = jnp.where(pick == 1, segs[5 + 2 * r], SCORE_FLOOR)
        scores = jnp.concatenate(segs + [scores[own_rows:]], axis=0)
        highest = jnp.max(scores, axis=0, keepdims=True)
        raw = jnp.exp(scores - highest)
        inverse = 1.0 / jnp.sum(raw, axis=0, keepdims=True)
        inner = jnp.sum(raw * grads, axis=0, keepdims=True) * inverse
        probs = raw * inverse
        grad_scores = probs * (grads - inner)
        packed = jnp.concatenate(
            [grad_scores.astype(jnp.bfloat16), probs.astype(jnp.bfloat16)], axis=1
        )
        terms = jnp.dot(packed[:own_rows], both, preferred_element_type=jnp.float32)
        out = lax.dot_general(
            keys, packed, (((0,), (0,)), ((), ())), preferred_element_type=jnp.float32
        )
        out = jnp.concatenate(
            [out[:HEAD_DIM, :SLAB] * 0.125, out[HEAD_DIM:, SLAB:]], axis=0
        )
        o_send[c] = out.T.astype(jnp.bfloat16)
        places = [before, 2 * c, 2 * c + 1, after]
        for r in range(RAND):
            other = partner(c, r)
            places += [2 * other, 2 * other + 1]
        return places, terms

    def add_terms(places, terms):
        for i, place in enumerate(places):
            acc[place] += terms[i * BLOCK : (i + 1) * BLOCK]

    def arrive_b(c):
        @pl.when(c != me)
        def _():
            send_b(me, c).wait_recv()

    def return_o(c):
        @pl.when((c != me) & (c % share == my_turn))
        def _():
            send_o(c, my_head).start()

        @pl.when(c == me)
        def _():
            o_all[my_head] = o_send[me]

    def return_d(c):
        @pl.when((c != me) & (c % share == my_turn))
        def _():
            total = acc[pl.ds(2 * c, 2)].reshape(SLAB, PACK)
            d_send[c] = total.astype(jnp.bfloat16)
            send_d(c, my_head).start()

        @pl.when(c == me)
        def _():
            total = acc[pl.ds(2 * me, 2)].reshape(SLAB, PACK)
            d_all[my_head] = total.astype(jnp.bfloat16)

    steps = half_n // 2

    def place_of(j, odd):
        return 2 * ((spot // 2 + steps - j) % steps) + odd

    def two_slabs(first, second):
        arrive_b(first)
        arrive_b(second)
        done = [slab(first), slab(second)]
        for places, terms in done:
            add_terms(places, terms)
        return_o(first)
        return_o(second)

    def both_sides(act, place):
        act((1 - side) * half_n + place)
        act(side * half_n + place)

    def even_step(t, carry):
        place = place_of(t, 0)
        two_slabs((1 - side) * half_n + place, side * half_n + place)
        return carry

    lax.fori_loop(0, steps, even_step, 0)

    def odd_step(t, carry):
        place = place_of(t, 1)
        two_slabs((1 - side) * half_n + place, side * half_n + place)

        @pl.when(t > 0)
        def _():
            both_sides(return_d, (place + 1) % half_n)

        return carry

    lax.fori_loop(0, steps, odd_step, 0)
    both_sides(return_d, (place_of(0, 1) + 1) % half_n)

    def return_odd(t, carry):
        both_sides(return_d, place_of(t, 1))
        return carry

    lax.fori_loop(0, steps, return_odd, 0)

    def arrive_o(i, carry):
        send_o(me, (my_head + i) % HEADS).wait_recv()
        return carry

    lax.fori_loop(1, HEADS, arrive_o, 0)

    def unpack(source, low_ref, high_ref):
        for pair in range(HEADS // 2):
            cols = slice(PACK * pair, PACK * (pair + 1))
            even, odd = source[2 * pair], source[2 * pair + 1]
            low_ref[:, cols] = jnp.concatenate(
                [even[:, :HEAD_DIM], odd[:, :HEAD_DIM]], axis=1
            )
            high_ref[:, cols] = jnp.concatenate(
                [even[:, HEAD_DIM:], odd[:, HEAD_DIM:]], axis=1
            )

    unpack(o_all, dq_ref, att_ref)

    def arrive_d(i, carry):
        send_d(me, (my_head + i) % HEADS).wait_recv()
        return carry

    lax.fori_loop(1, HEADS, arrive_d, 0)
    unpack(d_all, dk_ref, dv_ref)

    def sent_in(i, carry):
        send_a((me + i) % n, me).wait_send()
        send_b((me + i) % n, me).wait_send()
        send_c((me + i) % n, me).wait_send()
        return carry

    lax.fori_loop(1, n, sent_in, 0)

    def sent_back(i, carry):
        c = ((my_head + HEADS - i) % HEADS) * share + my_turn
        send_o(c, my_head).wait_send()
        send_d(c, my_head).wait_send()
        return carry

    lax.fori_loop(1, HEADS, sent_back, 0)


def local(n, queries, keys, values, grad_out, rand_blocks, global_ids):
    out = jax.ShapeDtypeStruct(queries.shape, jnp.bfloat16)
    vmem = pl.BlockSpec(memory_space=pltpu.VMEM)
    dma = pltpu.SemaphoreType.DMA
    return pl.pallas_call(
        functools.partial(kernel, n),
        out_shape=(out,) * 4,
        in_specs=[pl.BlockSpec(memory_space=pl.ANY)] * 6,
        out_specs=(vmem,) * 4,
        scratch_shapes=[
            pltpu.VMEM(queries.shape, jnp.bfloat16),
            pltpu.VMEM(queries.shape, jnp.bfloat16),
            pltpu.VMEM(queries.shape, jnp.bfloat16),
            pltpu.VMEM(queries.shape, jnp.bfloat16),
            pltpu.SMEM(rand_blocks.shape, jnp.int32),
            pltpu.SMEM(global_ids.shape, jnp.int32),
            dma((6,)),
            pltpu.VMEM((HEADS, 2, BLOCK, PACK), jnp.bfloat16),
            pltpu.VMEM((HEADS, SLAB, PACK), jnp.bfloat16),
            pltpu.VMEM((2 * n, BLOCK, PACK), jnp.bfloat16),
            pltpu.VMEM((n, SLAB, PACK), jnp.bfloat16),
            pltpu.VMEM((2 * n, BLOCK, PACK), jnp.float32),
            pltpu.VMEM((n, SLAB, PACK), jnp.bfloat16),
            pltpu.VMEM((HEADS, SLAB, PACK), jnp.bfloat16),
            pltpu.VMEM((n, SLAB, PACK), jnp.bfloat16),
            pltpu.VMEM((HEADS, SLAB, PACK), jnp.bfloat16),
            pltpu.VMEM((1, PACK), jnp.float32),
            pltpu.VMEM((n, 1, PACK), jnp.float32),
            dma((n,)),
            dma((n,)),
            dma((n,)),
            dma((n,)),
            dma((n,)),
            dma((n,)),
            dma((n,)),
            dma((HEADS,)),
            dma((n,)),
            dma((HEADS,)),
        ],
        compiler_params=pltpu.CompilerParams(
            collective_id=0, has_side_effects=True, vmem_limit_bytes=63 * 1024 * 1024
        ),
    )(queries, keys, values, grad_out, rand_blocks, global_ids)


def solution(mesh):
    rows = P(("dp", "ctx"), None)
    return jax.shard_map(
        functools.partial(local, mesh.shape["ctx"]),
        mesh=mesh,
        in_specs=(rows,) * 5 + (P("dp"),),
        out_specs=(rows,) * 4,
        check_vma=False,
    )
```
